32 devices in a mesh: dp: 4 (over y, x), space: 8 (over z, core).
Axes of the slice: x: 2, y: 2, z: 4, core: 2. Of those that a mesh axis runs over, the one named last changes fastest.
Arguments:
- volumes: bfloat16 [4, 32, 16, 48, 128], P('dp', None, 'space'), may hold values from -6 to 6
- kernel: bfloat16 [3, 3, 3, 64, 32], replicated, may hold values from -0.21875 to 0.21875
- bias: float32 [64], replicated, may hold values from -3 to 3
- cotangent: bfloat16 [4, 64, 16, 48, 128], P('dp', None, 'space'), may hold values from -6 to 6
- finished_grads: float32 [4, 8, 262144], P('dp', 'space'), may hold values from -0.5 to 0.5
Outputs:
- activations: bfloat16 [4, 64, 16, 48, 128], P('dp', None, 'space')
- grad_volumes: bfloat16 [4, 32, 16, 48, 128], P('dp', None, 'space')
- grad_kernel: float32 [3, 3, 3, 64, 32], replicated
- grad_bias: float32 [64], replicated
- summed_grads: float32 [262144], replicated
The draws below stay inside these ranges and needn't reach their ends.
All inputs are finite; a program needn't handle non-finite values.
Results may differ from the reference program's by a relative error of at most 0.006.
Values may be sent and summed in bfloat16 or wider, within the bound.
A program may use at most 128 MiB of HBM per device.

```python
import math
import jax
import jax.numpy as jnp
from jax import lax

C_IN = 32
C_OUT = 64
CY = 48
CX = 128
GRADS = 262144
BATCH = 4
NZ = 16
N_DP = 4
N_SPACE = 8


def block_scale(key, extent, shards, low, largest):
    def one(axis_at, blocks):
        steps = jax.random.uniform(jax.random.fold_in(jax.random.fold_in(key, 6), axis_at), (blocks,), jnp.float32, low / len(shards), largest / len(shards))
        return jnp.repeat(jnp.exp(steps), extent[axis_at] // blocks).reshape((-1,) + (1,) * (len(extent) - axis_at - 1))

    gain = one(*shards[0])
    for cut in shards[1:]:
        gain = gain * one(*cut)
    return gain


def gaussian(rng, extent, scale, limit, shards=(), held_as=jnp.bfloat16):
    array = scale * jax.random.normal(rng, extent, jnp.float32)
    if shards:
        array = array * block_scale(rng, extent, shards, -0.22, 0.18)
    return jnp.clip(array, -limit, limit).astype(held_as)


def setup_inputs(seed: int = 0) -> dict:
    key_list = jax.random.split(jax.random.key(seed), 6)
    volumes = gaussian(key_list[0], (BATCH, C_IN, NZ, CY, CX), 1.0, 6.0, ((0, 4), (2, 8)))
    kernel = gaussian(key_list[1], (3, 3, 3, C_OUT, C_IN), (27 * C_IN) ** -0.5, 0.21875)
    bias = gaussian(key_list[2], (C_OUT,), 0.5, 3.0, (), jnp.float32)
    cotangent = gaussian(key_list[3], (BATCH, C_OUT, NZ, CY, CX), 1.0, 6.0, ((0, 4), (2, 8)))
    finished_grads = gaussian(key_list[4], (N_DP, N_SPACE, GRADS), 0.0625, 0.5, ((0, 4), (1, 8)), jnp.float32)
    return {"volumes": volumes, "kernel": kernel, "bias": bias, "cotangent": cotangent, "finished_grads": finished_grads}


def convolve(field, weights):
    return lax.conv_general_dilated(field[None], weights, (1, 1, 1), [(1, 1), (1, 1), (1, 1)], dimension_numbers=('NCDHW', 'OIDHW', 'NCDHW'), preferred_element_type=jnp.float32)[0]

def reference(volumes, kernel, bias, cotangent, finished_grads):
    forward_w = kernel.transpose(3, 4, 0, 1, 2)
    backward_w = kernel[::-1, ::-1, ::-1].transpose(4, 3, 0, 1, 2)

    def one_sample(pair):
        volume, cot_one = pair
        preact = convolve(volume, forward_w) + bias[:, None, None, None]
        activation = (0.3 * preact + 0.7 * jax.nn.softplus(preact)).astype(jnp.bfloat16)
        grad_pre = (cot_one.astype(jnp.float32) * (0.3 + 0.7 * jax.nn.sigmoid(preact))).astype(jnp.bfloat16)
        grad_input = convolve(grad_pre, backward_w).astype(jnp.bfloat16)
        padded = jnp.pad(volume, ((0, 0), (1, 1), (1, 1), (1, 1)))
        grad_flat = grad_pre.reshape(C_OUT, -1)
        taps = []
        for depth_tap in range(3):
            for row_tap in range(3):
                for col_tap in range(3):
                    shifted = padded[:, depth_tap:depth_tap + NZ, row_tap:row_tap + CY, col_tap:col_tap + CX].reshape(C_IN, -1)
                    taps.append(jnp.dot(grad_flat, shifted.T, preferred_element_type=jnp.float32))
        grad_taps = jnp.stack(taps).reshape(3, 3, 3, C_OUT, C_IN)
        bias_terms = lax.optimization_barrier(jnp.sum(grad_pre.astype(jnp.float32), axis=(1, 2, 3)))
        return (activation, grad_input, grad_taps, bias_terms)
    activations, grad_volumes, grad_taps, bias_terms = lax.map(one_sample, (volumes, cotangent))
    scale = 1.0 / math.sqrt(BATCH * NZ * CY * CX)
    grad_kernel = lax.optimization_barrier(jnp.sum(grad_taps, axis=0)) * scale
    grad_bias = lax.optimization_barrier(jnp.sum(bias_terms, axis=0)) * scale
    summed_grads = lax.optimization_barrier(jnp.sum(finished_grads, axis=(0, 1)))
    return (activations, grad_volumes, grad_kernel, grad_bias, summed_grads)
```

```python
import functools
import math

import jax
import jax.numpy as jnp
from jax import lax
from jax.experimental import pallas as pl
from jax.experimental.pallas import tpu as pltpu
from jax.sharding import PartitionSpec as P

VMEM = pl.BlockSpec(memory_space=pltpu.VMEM)
STEP = 2


def spread(block):
    wide = block.astype(jnp.float32)
    columns = wide.shape[1]
    lane = lax.broadcasted_iota(jnp.int32, wide.shape, 1)
    right = jnp.where(lane == 0, 0.0, pltpu.roll(wide, 1, 1))
    left = jnp.where(lane == columns - 1, 0.0, pltpu.roll(wide, columns - 1, 1))
    return right.astype(block.dtype), block, left.astype(block.dtype)


def fill(taps, plane, row, block):
    channels = block.shape[0]
    for k, part in enumerate(spread(block)):
        taps[plane, row + 1, k * channels : (k + 1) * channels, :] = part


def clear_rim(taps):
    planes, rows, depth, columns = taps.shape
    for plane in range(planes):
        for row in (0, rows - 1):
            taps[plane, row] = jnp.zeros((depth, columns), taps.dtype)


def patch(taps, row):
    planes, _, depth, columns = taps.shape
    tall = []
    for plane in range(planes):
        tall.append(
            jnp.concatenate(
                [
                    taps[plane, pl.ds(row + r, 3)].reshape(3 * depth, columns)
                    for r in range(STEP)
                ],
                axis=1,
            )
        )
    return jnp.concatenate(tall, axis=0)


def forward_kernel(lo, mid, hi, w, bias, cot, act, gp, gk, gb, taps):
    depth, rows, channels, columns = mid.shape
    outs = cot.shape[2]
    clear_rim(taps)

    @pl.loop(0, rows)
    def _(row):
        fill(taps, 0, row, lo[row])
        for z in range(depth):
            fill(taps, z + 1, row, mid[z, row])
        fill(taps, depth + 1, row, hi[row])

    gk[...] = jnp.zeros_like(gk)
    gb[...] = jnp.zeros_like(gb)

    @pl.loop(0, rows // STEP)
    def _(step):
        row = step * STEP
        cells = patch(taps, row)
        pre = jnp.dot(w[...], cells, preferred_element_type=jnp.float32) + bias[...]
        grads = []
        for z in range(depth):
            line = []
            for r in range(STEP):
                v = pre[z * outs : (z + 1) * outs, r * columns : (r + 1) * columns]
                e = jnp.exp(-jnp.abs(v))
                soft = jnp.maximum(v, 0.0) + jnp.log(1.0 + e)
                sig = jnp.where(v >= 0.0, 1.0, e) / (1.0 + e)
                act[z, row + r] = (0.3 * v + 0.7 * soft).astype(act.dtype)
                g = (cot[z, row + r].astype(jnp.float32) * (0.3 + 0.7 * sig)).astype(gp.dtype)
                gp[z, row + r] = g
                gb[...] += g.astype(jnp.float32)
                line.append(g)
            grads.append(jnp.concatenate(line, axis=1))
        grad = jnp.concatenate(grads, axis=0)
        gk[...] += lax.dot_general(
            cells, grad, (((1,), (1,)), ((), ())), preferred_element_type=jnp.float32
        )


def backward_kernel(lo, mid, hi, w, out, taps):
    depth, rows, channels, columns = mid.shape
    ins = out.shape[2]
    clear_rim(taps)

    @pl.loop(0, rows)
    def _(row):
        fill(taps, 0, row, lo[row])
        for z in range(depth):
            fill(taps, z + 1, row, mid[z, row])
        fill(taps, depth + 1, row, hi[row])

    @pl.loop(0, rows // STEP)
    def _(step):
        row = step * STEP
        cells = patch(taps, row)
        res = jnp.dot(w[...], cells, preferred_element_type=jnp.float32)
        for z in range(depth):
            for r in range(STEP):
                out[z, row + r] = res[
                    z * ins : (z + 1) * ins, r * columns : (r + 1) * columns
                ].astype(out.dtype)


def banded(w, depth):
    outs, width = w.shape[1:]
    flat = w.transpose(1, 0, 2).reshape(outs, 3 * width)
    lines = [
        jnp.pad(flat, ((0, 0), (z * width, (depth - 1 - z) * width))) for z in range(depth)
    ]
    return jnp.concatenate(lines, axis=0)


def neighbours(planes):
    count = lax.axis_size("space")
    up = [(i, i + 1) for i in range(count - 1)]
    down = [(i + 1, i) for i in range(count - 1)]
    lo = lax.ppermute(planes[-1], "space", up)
    hi = lax.ppermute(planes[0], "space", down)
    return lo, hi


def local(volumes, kernel, bias, cotangent, finished_grads):
    volume = volumes[0].transpose(1, 2, 0, 3)
    cot = cotangent[0].transpose(1, 2, 0, 3)
    depth, rows, ins, columns = volume.shape
    outs = cot.shape[2]
    planes = depth + 2
    limit = pltpu.CompilerParams(vmem_limit_bytes=48 * 2**20)
    lo, hi = neighbours(volume)
    forward_w = banded(kernel.transpose(0, 3, 1, 2, 4).reshape(3, outs, 9 * ins), depth)
    backward_w = banded(
        kernel[::-1, ::-1, ::-1].transpose(0, 4, 1, 2, 3).reshape(3, ins, 9 * outs), depth
    )
    tall_bias = jnp.tile(bias, depth)[:, None]
    act, gp, gk, gb = pl.pallas_call(
        forward_kernel,
        out_shape=(
            jax.ShapeDtypeStruct((depth, rows, outs, columns), jnp.bfloat16),
            jax.ShapeDtypeStruct((depth, rows, outs, columns), jnp.bfloat16),
            jax.ShapeDtypeStruct((planes * 9 * ins, depth * outs), jnp.float32),
            jax.ShapeDtypeStruct((outs, columns), jnp.float32),
        ),
        in_specs=[VMEM] * 6,
        out_specs=(VMEM,) * 4,
        scratch_shapes=[pltpu.VMEM((planes, rows + 2, 3 * ins, columns), jnp.bfloat16)],
        compiler_params=limit,
        name="forward",
    )(lo, volume, hi, forward_w, tall_bias, cot)
    glo, ghi = neighbours(gp)
    gvol = pl.pallas_call(
        backward_kernel,
        out_shape=jax.ShapeDtypeStruct((depth, rows, ins, columns), jnp.bfloat16),
        in_specs=[VMEM] * 4,
        out_specs=VMEM,
        scratch_shapes=[pltpu.VMEM((planes, rows + 2, 3 * outs, columns), jnp.bfloat16)],
        compiler_params=limit,
        name="backward",
    )(glo, gp, ghi, backward_w)
    full = gk.reshape(planes, 3, 3, ins, depth, outs)
    taps = sum(full[z : z + 3, :, :, :, z] for z in range(depth)).transpose(0, 1, 2, 4, 3)
    bias_terms = jnp.sum(gb, axis=1)
    small = jnp.concatenate([taps.reshape(-1), bias_terms])
    summed = lax.psum(finished_grads.reshape(-1), ("dp", "space"))
    total = lax.psum(small, ("dp", "space"))
    count = lax.axis_size("dp") * lax.axis_size("space") * depth * rows * columns
    scale = 1.0 / math.sqrt(count)
    total = total * scale
    activations = act.transpose(2, 0, 1, 3)[None]
    grad_volumes = gvol.transpose(2, 0, 1, 3)[None]
    return (
        activations,
        grad_volumes,
        total[: taps.size].reshape(taps.shape),
        total[taps.size :],
        summed,
    )


def solution(mesh):
    slab = P("dp", None, "space", None, None)
    return jax.shard_map(
        local,
        mesh=mesh,
        in_specs=(slab, P(), P(), slab, P("dp", "space", None)),
        out_specs=(slab, slab, P(), P(), P()),
        check_vma=False,
    )
```

```python
import functools
import math

import jax
import jax.numpy as jnp
from jax import lax
from jax.experimental import pallas as pl
from jax.experimental.pallas import tpu as pltpu
from jax.sharding import PartitionSpec as P

VMEM = pl.BlockSpec(memory_space=pltpu.VMEM)
STEP = 2
FORWARD_AT = ((1, 0), (2, 9), (3, 13), (4, 17))
BACKWARD_AT = ((1, 0), (2, 5), (3, 10), (4, 15), (5, 20))


def spread(block):
    wide = block.astype(jnp.float32)
    columns = wide.shape[1]
    lane = lax.broadcasted_iota(jnp.int32, wide.shape, 1)
    right = jnp.where(lane == 0, 0.0, pltpu.roll(wide, 1, 1))
    left = jnp.where(lane == columns - 1, 0.0, pltpu.roll(wide, columns - 1, 1))
    return right.astype(block.dtype), block, left.astype(block.dtype)


def fill(taps, plane, row, block):
    channels = block.shape[0]
    for k, part in enumerate(spread(block)):
        taps[plane, row + 1, k * channels : (k + 1) * channels, :] = part


def clear_rim(taps):
    planes, rows, depth, columns = taps.shape
    for plane in range(planes):
        for row in (0, rows - 1):
            taps[plane, row] = jnp.zeros((depth, columns), taps.dtype)


def patch(taps, row):
    planes, _, depth, columns = taps.shape
    tall = []
    for plane in range(planes):
        tall.append(
            jnp.concatenate(
                [
                    taps[plane, pl.ds(row + r, 3)].reshape(3 * depth, columns)
                    for r in range(STEP)
                ],
                axis=1,
            )
        )
    return jnp.concatenate(tall, axis=0)


def ring_sizes():
    return 2, lax.axis_size("dp"), lax.axis_size("space") // 2


def copies_per_sum():
    pair, line, deep = ring_sizes()
    return 2 * (pair - 1 + line - 1 + deep - 1)


def sum_scratch(rows, columns):
    pair, line, deep = ring_sizes()
    return [
        pltpu.VMEM((line, deep, rows, columns), jnp.float32),
        pltpu.VMEM((line - 1, deep, rows, columns), jnp.float32),
        pltpu.VMEM((deep, rows, columns), jnp.float32),
        pltpu.VMEM((deep - 1, rows, columns), jnp.float32),
        pltpu.VMEM((pair, line, deep, rows, columns), jnp.float32),
        pltpu.SemaphoreType.DMA((copies_per_sum(),)),
        pltpu.SemaphoreType.DMA((copies_per_sum(),)),
    ]


class SumStages:
    def __init__(self, x, total, half, from_line, quarter, from_deep, full, sends, recvs):
        self.x, self.total, self.half, self.from_line = x, total, half, from_line
        self.quarter, self.from_deep, self.full = quarter, from_deep, full
        self.sends, self.recvs = sends, recvs
        self.pair, self.line, self.deep = ring_sizes()
        self.dp = lax.axis_index("dp")
        space = lax.axis_index("space")
        self.core, self.z = lax.rem(space, 2), space // 2
        self.partners = [(self.dp, self.z * 2 + 1 - self.core)]
        self.lines = [lax.rem(self.dp + t, self.line) for t in range(1, self.line)]
        self.deeps = [lax.rem(self.z + t, self.deep) for t in range(1, self.deep)]
        self.partners += [(p, space) for p in self.lines]
        self.partners += [(self.dp, p * 2 + self.core) for p in self.deeps]

    def greet(self):
        barrier = pltpu.get_barrier_semaphore()
        for other in self.partners:
            pl.semaphore_signal(
                barrier, inc=1, device_id=other, device_id_type=pl.DeviceIdType.MESH
            )
        pl.semaphore_wait(barrier, len(self.partners))

    def copy(self, source, target, slot, other):
        return pltpu.make_async_remote_copy(
            src_ref=source,
            dst_ref=target,
            send_sem=self.sends.at[slot],
            recv_sem=self.recvs.at[slot],
            device_id=self.partners[other],
            device_id_type=pl.DeviceIdType.MESH,
        )

    def moves(self, stage):
        first_line, first_deep, second = 1, self.line, self.line + self.deep - 1
        mine = self.full.at[self.core]
        if stage == 0:
            return [self.copy(self.x.at[1 - self.core], self.half, 0, 0)]
        if stage == 1:
            return [
                self.copy(self.half.at[p], self.from_line.at[t], first_line + t, first_line + t)
                for t, p in enumerate(self.lines)
            ]
        if stage == 2:
            return [
                self.copy(self.quarter.at[p], self.from_deep.at[t], first_deep + t, first_deep + t)
                for t, p in enumerate(self.deeps)
            ]
        if stage == 3:
            own = mine.at[self.dp, self.z]
            return [
                self.copy(own, own, second + first_deep + t, first_deep + t)
                for t in range(len(self.deeps))
            ]
        if stage == 4:
            own = mine.at[self.dp]
            return [
                self.copy(own, own, second + first_line + t, first_line + t)
                for t in range(len(self.lines))
            ]
        return [self.copy(mine, mine, second, 0)]

    def run(self, stage):
        if stage > 0:
            for move in self.moves(stage - 1):
                move.wait()
        if stage == 1:
            self.half[...] += self.x[self.core]
        if stage == 2:
            value = self.half[self.dp]
            for t in range(len(self.lines)):
                value += self.from_line[t]
            self.quarter[...] = value
        if stage == 3:
            value = self.quarter[self.z]
            for t in range(len(self.deeps)):
                value += self.from_deep[t]
            self.full[self.core, self.dp, self.z] = value
        if stage < 6:
            for move in self.moves(stage):
                move.start()
        else:
            self.total[...] = self.full[...]


def forward_kernel(lo, mid, hi, w, bias, cot, x, act, gp, small, total, taps, gk, *scratch):
    depth, rows, channels, columns = mid.shape
    outs = cot.shape[2]
    plane = 9 * channels
    stages = SumStages(x, total, *scratch)
    stages.greet()
    stages.run(0)
    clear_rim(taps)

    @pl.loop(0, rows)
    def _(row):
        fill(taps, 0, row, lo[row])
        for z in range(depth):
            fill(taps, z + 1, row, mid[z, row])
        fill(taps, depth + 1, row, hi[row])

    gk[...] = jnp.zeros_like(gk)
    steps = rows // STEP

    @pl.loop(0, steps)
    def _(step):
        for stage, at in FORWARD_AT:

            @pl.when(step == steps * at // 24)
            def _():
                stages.run(stage)

        row = step * STEP
        cells = patch(taps, row)
        pre = jnp.dot(w[...], cells, preferred_element_type=jnp.float32) + bias[...]
        grads = []
        for z in range(depth):
            line = []
            for r in range(STEP):
                v = pre[z * outs : (z + 1) * outs, r * columns : (r + 1) * columns]
                e = jnp.exp(-jnp.abs(v))
                soft = jnp.maximum(v, 0.0) + jnp.log(1.0 + e)
                sig = jnp.where(v >= 0.0, 1.0, e) / (1.0 + e)
                act[z, row + r] = (0.3 * v + 0.7 * soft).astype(act.dtype)
                g = (cot[z, row + r].astype(jnp.float32) * (0.3 + 0.7 * sig)).astype(gp.dtype)
                gp[z, row + r] = g
                line.append(g)
            grads.append(jnp.concatenate(line, axis=1))
        grad = jnp.concatenate(grads, axis=0)
        ones = jnp.ones((16, STEP * columns), cells.dtype)
        gk[...] += lax.dot_general(
            jnp.concatenate([cells, ones], axis=0),
            grad,
            (((1,), (1,)), ((), ())),
            preferred_element_type=jnp.float32,
        )

    small[...] = jnp.zeros_like(small)
    tall = 3 * plane
    ends = (depth + 2) * plane
    value = gk[0:tall, 0:outs]
    extra = gk[ends : ends + 8, 0:outs]
    for z in range(1, depth):
        value += gk[z * plane : z * plane + tall, z * outs : (z + 1) * outs]
        extra += gk[ends : ends + 8, z * outs : (z + 1) * outs]
    small[0 : tall // 2, :] = jnp.concatenate([value[: tall // 2], value[tall // 2 :]], axis=1)
    small[tall // 2 : tall // 2 + 8, :] = jnp.concatenate([extra, extra], axis=1)
    stages.run(5)
    stages.run(6)


def backward_kernel(lo, mid, hi, w, x, out, total, taps, *scratch):
    depth, rows, channels, columns = mid.shape
    ins = out.shape[2]
    stages = SumStages(x, total, *scratch)
    stages.greet()
    stages.run(0)
    clear_rim(taps)

    @pl.loop(0, rows)
    def _(row):
        fill(taps, 0, row, lo[row])
        for z in range(depth):
            fill(taps, z + 1, row, mid[z, row])
        fill(taps, depth + 1, row, hi[row])

    steps = rows // STEP

    @pl.loop(0, steps)
    def _(step):
        for stage, at in BACKWARD_AT:

            @pl.when(step == steps * at // 24)
            def _():
                stages.run(stage)

        row = step * STEP
        cells = patch(taps, row)
        res = jnp.dot(w[...], cells, preferred_element_type=jnp.float32)
        for z in range(depth):
            for r in range(STEP):
                out[z, row + r] = res[
                    z * ins : (z + 1) * ins, r * columns : (r + 1) * columns
                ].astype(out.dtype)

    stages.run(6)


def banded(w, depth):
    outs, width = w.shape[1:]
    flat = w.transpose(1, 0, 2).reshape(outs, 3 * width)
    lines = [
        jnp.pad(flat, ((0, 0), (z * width, (depth - 1 - z) * width))) for z in range(depth)
    ]
    return jnp.concatenate(lines, axis=0)


def neighbours(planes):
    count = lax.axis_size("space")
    up = [(i, i + 1) for i in range(count - 1)]
    down = [(i + 1, i) for i in range(count - 1)]
    lo = lax.ppermute(planes[-1], "space", up)
    hi = lax.ppermute(planes[0], "space", down)
    return lo, hi


def local(volumes, kernel, bias, cotangent, finished_grads):
    volume = volumes[0].transpose(1, 2, 0, 3)
    cot = cotangent[0].transpose(1, 2, 0, 3)
    depth, rows, ins, columns = volume.shape
    outs = cot.shape[2]
    planes = depth + 2
    lo, hi = neighbours(volume)
    forward_w = banded(kernel.transpose(0, 3, 1, 2, 4).reshape(3, outs, 9 * ins), depth)
    backward_w = banded(
        kernel[::-1, ::-1, ::-1].transpose(0, 4, 1, 2, 3).reshape(3, ins, 9 * outs), depth
    )
    tall_bias = jnp.tile(bias, depth)[:, None]
    sizes = ring_sizes()
    devices = math.prod(sizes)

    def share(count):
        return 8 * math.ceil(count / (columns * devices * 8))

    entries = finished_grads.size
    parts = share(entries)
    flat = jnp.pad(finished_grads.reshape(-1), (0, parts * columns * devices - entries))
    tall = 27 * ins // 2
    small_parts = share((tall + 8) * columns)
    act, gp, small, summed = pl.pallas_call(
        forward_kernel,
        out_shape=(
            jax.ShapeDtypeStruct((depth, rows, outs, columns), jnp.bfloat16),
            jax.ShapeDtypeStruct((depth, rows, outs, columns), jnp.bfloat16),
            jax.ShapeDtypeStruct((small_parts * devices, columns), jnp.float32),
            jax.ShapeDtypeStruct((*sizes, parts, columns), jnp.float32),
        ),
        in_specs=[VMEM] * 7,
        out_specs=(VMEM,) * 4,
        scratch_shapes=[
            pltpu.VMEM((planes, rows + 2, 3 * ins, columns), jnp.bfloat16),
            pltpu.VMEM((planes * 9 * ins + 16, depth * outs), jnp.float32),
            *sum_scratch(parts, columns),
        ],
        compiler_params=pltpu.CompilerParams(
            vmem_limit_bytes=48 * 2**20, collective_id=0, has_side_effects=True
        ),
        name="forward",
    )(lo, volume, hi, forward_w, tall_bias, cot, flat.reshape(*sizes, parts, columns))
    glo, ghi = neighbours(gp)
    gvol, small_sum = pl.pallas_call(
        backward_kernel,
        out_shape=(
            jax.ShapeDtypeStruct((depth, rows, ins, columns), jnp.bfloat16),
            jax.ShapeDtypeStruct((*sizes, small_parts, columns), jnp.float32),
        ),
        in_specs=[VMEM] * 5,
        out_specs=(VMEM,) * 2,
        scratch_shapes=[
            pltpu.VMEM((planes, rows + 2, 3 * outs, columns), jnp.bfloat16),
            *sum_scratch(small_parts, columns),
        ],
        compiler_params=pltpu.CompilerParams(
            vmem_limit_bytes=48 * 2**20, collective_id=1, has_side_effects=True
        ),
        name="backward",
    )(glo, gp, ghi, backward_w, small.reshape(*sizes, small_parts, columns))
    count = lax.axis_size("dp") * lax.axis_size("space") * depth * rows * columns
    scale = 1.0 / math.sqrt(count)
    lines = small_sum.reshape(-1, columns)
    halves = [lines[:tall, h * outs : (h + 1) * outs] for h in range(2)]
    taps = jnp.concatenate(halves, axis=0).reshape(3, 3, 3, ins, outs)
    activations = act.transpose(2, 0, 1, 3)[None]
    grad_volumes = gvol.transpose(2, 0, 1, 3)[None]
    return (
        activations,
        grad_volumes,
        taps.transpose(0, 1, 2, 4, 3) * scale,
        lines[tall, :outs] * scale,
        summed.reshape(-1)[:entries],
    )


def solution(mesh):
    slab = P("dp", None, "space", None, None)
    return jax.shard_map(
        local,
        mesh=mesh,
        in_specs=(slab, P(), P(), slab, P("dp", "space", None)),
        out_specs=(slab, slab, P(), P(), P()),
        check_vma=False,
    )
```

```python
import functools
import math

import jax
import jax.numpy as jnp
from jax import lax
from jax.experimental import pallas as pl
from jax.experimental.pallas import tpu as pltpu
from jax.sharding import PartitionSpec as P

VMEM = pl.BlockSpec(memory_space=pltpu.VMEM)
STEP = 2
PARTS = 4
FORWARD_AT = ((1, 1), (2, 11), (3, 16), (4, 20))
WIDE_AT = ((5, 6),)
BACKWARD_AT = ((1, 0), (2, 5), (3, 10), (4, 15), (5, 20))


def spread(block):
    wide = block.astype(jnp.float32)
    columns = wide.shape[1]
    lane = lax.broadcasted_iota(jnp.int32, wide.shape, 1)
    right = jnp.where(lane == 0, 0.0, pltpu.roll(wide, 1, 1))
    left = jnp.where(lane == columns - 1, 0.0, pltpu.roll(wide, columns - 1, 1))
    return right.astype(block.dtype), block, left.astype(block.dtype)


def fill(taps, plane, row, block):
    channels = block.shape[0]
    for k, part in enumerate(spread(block)):
        taps[plane, row + 1, k * channels : (k + 1) * channels, :] = part


def clear_rim(taps):
    planes, rows, depth, columns = taps.shape
    for plane in range(planes):
        for row in (0, rows - 1):
            taps[plane, row] = jnp.zeros((depth, columns), taps.dtype)


def patch(taps, row):
    planes, _, depth, columns = taps.shape
    tall = []
    for plane in range(planes):
        tall.append(
            jnp.concatenate(
                [
                    taps[plane, pl.ds(row + r, 3)].reshape(3 * depth, columns)
                    for r in range(STEP)
                ],
                axis=1,
            )
        )
    return jnp.concatenate(tall, axis=0)


def ring_sizes():
    return 2, lax.axis_size("dp"), lax.axis_size("space") // 2


def copies_per_sum():
    pair, line, deep = ring_sizes()
    return 2 * (pair - 1 + line - 1 + deep - 1)


def sum_scratch(rows, columns):
    pair, line, deep = ring_sizes()
    return [
        pltpu.VMEM((line, deep, rows, columns), jnp.float32),
        pltpu.VMEM((line - 1, deep, rows, columns), jnp.float32),
        pltpu.VMEM((deep, rows, columns), jnp.float32),
        pltpu.VMEM((deep - 1, rows, columns), jnp.float32),
        pltpu.VMEM((pair, line, deep, rows, columns), jnp.float32),
        pltpu.SemaphoreType.DMA((copies_per_sum(),)),
        pltpu.SemaphoreType.DMA((copies_per_sum(),)),
    ]


class SumStages:
    def __init__(self, x, total, half, from_line, quarter, from_deep, full, sends, recvs):
        self.x, self.total, self.half, self.from_line = x, total, half, from_line
        self.quarter, self.from_deep, self.full = quarter, from_deep, full
        self.sends, self.recvs = sends, recvs
        self.pair, self.line, self.deep = ring_sizes()
        self.dp = lax.axis_index("dp")
        space = lax.axis_index("space")
        self.core, self.z = lax.rem(space, 2), space // 2
        self.partners = [(self.dp, self.z * 2 + 1 - self.core)]
        self.lines = [lax.rem(self.dp + t, self.line) for t in range(1, self.line)]
        self.deeps = [lax.rem(self.z + t, self.deep) for t in range(1, self.deep)]
        self.partners += [(p, space) for p in self.lines]
        self.partners += [(self.dp, p * 2 + self.core) for p in self.deeps]

    def greet(self, *more):
        barrier = pltpu.get_barrier_semaphore()
        others = [*self.partners, *more]
        for other in others:
            pl.semaphore_signal(
                barrier, inc=1, device_id=other, device_id_type=pl.DeviceIdType.MESH
            )
        pl.semaphore_wait(barrier, len(others))

    def copy(self, source, target, slot, other):
        return pltpu.make_async_remote_copy(
            src_ref=source,
            dst_ref=target,
            send_sem=self.sends.at[slot],
            recv_sem=self.recvs.at[slot],
            device_id=self.partners[other],
            device_id_type=pl.DeviceIdType.MESH,
        )

    def moves(self, stage):
        first_line, first_deep, second = 1, self.line, self.line + self.deep - 1
        mine = self.full.at[self.core]
        if stage == 0:
            return [self.copy(self.x.at[1 - self.core], self.half, 0, 0)]
        if stage == 1:
            return [
                self.copy(self.half.at[p], self.from_line.at[t], first_line + t, first_line + t)
                for t, p in enumerate(self.lines)
            ]
        if stage == 2:
            return [
                self.copy(self.quarter.at[p], self.from_deep.at[t], first_deep + t, first_deep + t)
                for t, p in enumerate(self.deeps)
            ]
        if stage == 3:
            own = mine.at[self.dp, self.z]
            return [
                self.copy(own, own, second + first_deep + t, first_deep + t)
                for t in range(len(self.deeps))
            ]
        if stage == 4:
            own = mine.at[self.dp]
            return [
                self.copy(own, own, second + first_line + t, first_line + t)
                for t in range(len(self.lines))
            ]
        return [self.copy(mine, mine, second, 0)]

    def run(self, stage):
        if stage > 0:
            for move in self.moves(stage - 1):
                move.wait()
        if stage == 1:
            self.half[...] += self.x[self.core]
        if stage == 2:
            value = self.half[self.dp]
            for t in range(len(self.lines)):
                value += self.from_line[t]
            self.quarter[...] = value
        if stage == 3:
            value = self.quarter[self.z]
            for t in range(len(self.deeps)):
                value += self.from_deep[t]
            self.full[self.core, self.dp, self.z] = value
        if stage < 6:
            for move in self.moves(stage):
                move.start()
        else:
            self.total[...] = self.full[...]


def fused_kernel(
    mid, w, back_w, bias, cot, x, act, out, small_total, total,
    taps, back_taps, gk, gp, lo, hi, glo, ghi, small,
    halo_sends, halo_recvs, grad_sends, grad_recvs, *scratch
):
    depth, rows, channels, columns = mid.shape
    outs = cot.shape[2]
    plane = 9 * channels
    steps = rows // STEP
    part = rows // PARTS
    space = lax.axis_index("space")
    dp = lax.axis_index("dp")
    last = lax.axis_size("space") - 1
    half = len(scratch) // 2
    wide = SumStages(x, total, *scratch[:half])
    late = SumStages(small, small_total, *scratch[half:])
    other = lax.rem(space + 2 * lax.rem(space, 2) + last, last + 1)
    wide.greet((dp, other))

    def push(source, target, send, recv, to):
        return pltpu.make_async_remote_copy(
            src_ref=source,
            dst_ref=target,
            send_sem=send,
            recv_sem=recv,
            device_id=(dp, to),
            device_id_type=pl.DeviceIdType.MESH,
        )

    def volume_down():
        return push(mid.at[0], hi, halo_sends.at[0], halo_recvs.at[0], space - 1)

    def volume_up():
        return push(mid.at[depth - 1], lo, halo_sends.at[1], halo_recvs.at[1], space + 1)

    def grad_down(n):
        at = pl.ds(n * part, part)
        return push(gp.at[0, at], ghi.at[at], grad_sends.at[0, n], grad_recvs.at[0, n], space - 1)

    def grad_up(n):
        at = pl.ds(n * part, part)
        return push(
            gp.at[depth - 1, at], glo.at[at], grad_sends.at[1, n], grad_recvs.at[1, n], space + 1
        )

    @pl.when(space > 0)
    def _():
        volume_down().start()

    @pl.when(space < last)
    def _():
        volume_up().start()

    wide.run(0)
    clear_rim(taps)
    clear_rim(back_taps)

    @pl.loop(0, rows)
    def _(row):
        for z in range(depth):
            fill(taps, z + 1, row, mid[z, row])

    def rim(target, plane_in, edge):
        @pl.when(space == (last if edge else 0))
        def _():
            plane_in[...] = jnp.zeros_like(plane_in)

        @pl.loop(0, rows)
        def _(row):
            fill(target, depth + 1 if edge else 0, row, plane_in[row])

    @pl.when(space > 0)
    def _():
        volume_down().wait_send()
        volume_up().wait_recv()

    @pl.when(space < last)
    def _():
        volume_up().wait_send()
        volume_down().wait_recv()

    rim(taps, lo, 0)
    rim(taps, hi, 1)
    gk[...] = jnp.zeros_like(gk)

    @pl.loop(0, steps)
    def _(step):
        for stage, at in FORWARD_AT:

            @pl.when(step == steps * at // 24)
            def _():
                wide.run(stage)

        row = step * STEP
        cells = patch(taps, row)
        pre = jnp.dot(w[...], cells, preferred_element_type=jnp.float32) + bias[...]
        grads = []
        for z in range(depth):
            line = []
            for r in range(STEP):
                v = pre[z * outs : (z + 1) * outs, r * columns : (r + 1) * columns]
                e = jnp.exp(-jnp.abs(v))
                soft = jnp.maximum(v, 0.0) + jnp.log(1.0 + e)
                sig = jnp.where(v >= 0.0, 1.0, e) / (1.0 + e)
                act[z, row + r] = (0.3 * v + 0.7 * soft).astype(act.dtype)
                g = (cot[z, row + r].astype(jnp.float32) * (0.3 + 0.7 * sig)).astype(gp.dtype)
                gp[z, row + r] = g
                fill(back_taps, z + 1, row + r, g)
                line.append(g)
            grads.append(jnp.concatenate(line, axis=1))
        grad = jnp.concatenate(grads, axis=0)
        ones = jnp.ones((16, STEP * columns), cells.dtype)
        gk[...] += lax.dot_general(
            jnp.concatenate([cells, ones], axis=0),
            grad,
            (((1,), (1,)), ((), ())),
            preferred_element_type=jnp.float32,
        )
        for n in range(PARTS):

            @pl.when(step == (n + 1) * steps // PARTS - 1)
            def _():
                @pl.when(space > 0)
                def _():
                    grad_down(n).start()

                @pl.when(space < last)
                def _():
                    grad_up(n).start()

    tall = 3 * plane
    ends = (depth + 2) * plane
    value = gk[0:tall, 0:outs]
    extra = gk[ends : ends + 8, 0:outs]
    for z in range(1, depth):
        value += gk[z * plane : z * plane + tall, z * outs : (z + 1) * outs]
        extra += gk[ends : ends + 8, z * outs : (z + 1) * outs]
    lines = small.size // columns
    small[...] = jnp.concatenate(
        [
            jnp.concatenate([value[: tall // 2], value[tall // 2 :]], axis=1),
            jnp.concatenate([extra, extra], axis=1),
            jnp.zeros((lines - tall // 2 - 8, columns), jnp.float32),
        ],
        axis=0,
    ).reshape(small.shape)
    late.run(0)

    @pl.when(space > 0)
    def _():
        for n in range(PARTS):
            grad_down(n).wait_send()
            grad_up(n).wait_recv()

    @pl.when(space < last)
    def _():
        for n in range(PARTS):
            grad_up(n).wait_send()
            grad_down(n).wait_recv()

    rim(back_taps, glo, 0)
    rim(back_taps, ghi, 1)

    @pl.loop(0, steps)
    def _(step):
        for stage, at in WIDE_AT:

            @pl.when(step == steps * at // 24)
            def _():
                wide.run(stage)

        for stage, at in BACKWARD_AT:

            @pl.when(step == steps * at // 24)
            def _():
                late.run(stage)

        row = step * STEP
        res = jnp.dot(back_w[...], patch(back_taps, row), preferred_element_type=jnp.float32)
        for z in range(depth):
            for r in range(STEP):
                out[z, row + r] = res[
                    z * channels : (z + 1) * channels, r * columns : (r + 1) * columns
                ].astype(out.dtype)

    wide.run(6)
    late.run(6)


def banded(w, depth):
    outs, width = w.shape[1:]
    flat = w.transpose(1, 0, 2).reshape(outs, 3 * width)
    lines = [
        jnp.pad(flat, ((0, 0), (z * width, (depth - 1 - z) * width))) for z in range(depth)
    ]
    return jnp.concatenate(lines, axis=0)


def local(volumes, kernel, bias, cotangent, finished_grads):
    volume = volumes[0].transpose(1, 2, 0, 3)
    cot = cotangent[0].transpose(1, 2, 0, 3)
    depth, rows, ins, columns = volume.shape
    outs = cot.shape[2]
    planes = depth + 2
    forward_w = banded(kernel.transpose(0, 3, 1, 2, 4).reshape(3, outs, 9 * ins), depth)
    backward_w = banded(
        kernel[::-1, ::-1, ::-1].transpose(0, 4, 1, 2, 3).reshape(3, ins, 9 * outs), depth
    )
    tall_bias = jnp.tile(bias, depth)[:, None]
    sizes = ring_sizes()
    devices = math.prod(sizes)

    def share(count):
        return 8 * math.ceil(count / (columns * devices * 8))

    entries = finished_grads.size
    parts = share(entries)
    flat = jnp.pad(finished_grads.reshape(-1), (0, parts * columns * devices - entries))
    tall = 27 * ins // 2
    small_parts = share((tall + 8) * columns)
    narrow = jnp.bfloat16
    act, gvol, small_sum, summed = pl.pallas_call(
        fused_kernel,
        out_shape=(
            jax.ShapeDtypeStruct(cot.shape, narrow),
            jax.ShapeDtypeStruct(volume.shape, narrow),
            jax.ShapeDtypeStruct((*sizes, small_parts, columns), jnp.float32),
            jax.ShapeDtypeStruct((*sizes, parts, columns), jnp.float32),
        ),
        in_specs=[VMEM] * 6,
        out_specs=(VMEM,) * 4,
        scratch_shapes=[
            pltpu.VMEM((planes, rows + 2, 3 * ins, columns), narrow),
            pltpu.VMEM((planes, rows + 2, 3 * outs, columns), narrow),
            pltpu.VMEM((planes * 9 * ins + 16, depth * outs), jnp.float32),
            pltpu.VMEM(cot.shape, narrow),
            pltpu.VMEM(volume.shape[1:], narrow),
            pltpu.VMEM(volume.shape[1:], narrow),
            pltpu.VMEM(cot.shape[1:], narrow),
            pltpu.VMEM(cot.shape[1:], narrow),
            pltpu.VMEM((*sizes, small_parts, columns), jnp.float32),
            pltpu.SemaphoreType.DMA((2,)),
            pltpu.SemaphoreType.DMA((2,)),
            pltpu.SemaphoreType.DMA((2, PARTS)),
            pltpu.SemaphoreType.DMA((2, PARTS)),
            *sum_scratch(parts, columns),
            *sum_scratch(small_parts, columns),
        ],
        compiler_params=pltpu.CompilerParams(
            vmem_limit_bytes=52 * 2**20, collective_id=0, has_side_effects=True
        ),
        name="fused",
    )(
        volume,
        forward_w,
        backward_w,
        tall_bias,
        cot,
        flat.reshape(*sizes, parts, columns),
    )
    count = lax.axis_size("dp") * lax.axis_size("space") * depth * rows * columns
    scale = 1.0 / math.sqrt(count)
    lines = small_sum.reshape(-1, columns)
    halves = [lines[:tall, h * outs : (h + 1) * outs] for h in range(2)]
    taps = jnp.concatenate(halves, axis=0).reshape(3, 3, 3, ins, outs)
    activations = act.transpose(2, 0, 1, 3)[None]
    grad_volumes = gvol.transpose(2, 0, 1, 3)[None]
    return (
        activations,
        grad_volumes,
        taps.transpose(0, 1, 2, 4, 3) * scale,
        lines[tall, :outs] * scale,
        summed.reshape(-1)[:entries],
    )


def solution(mesh):
    slab = P("dp", None, "space", None, None)
    return jax.shard_map(
        local,
        mesh=mesh,
        in_specs=(slab, P(), P(), slab, P("dp", "space", None)),
        out_specs=(slab, slab, P(), P(), P()),
        check_vma=False,
    )
```

```python
import functools
import math

import jax
import jax.numpy as jnp
from jax import lax
from jax.experimental import pallas as pl
from jax.experimental.pallas import tpu as pltpu
from jax.sharding import PartitionSpec as P

VMEM = pl.BlockSpec(memory_space=pltpu.VMEM)
STEP = 4
PARTS = 4
FORWARD_AT = ((1, 1), (2, 11), (3, 16), (4, 20))
WIDE_AT = ((5, 6),)
BACKWARD_AT = ((1, 0), (2, 5), (3, 10), (4, 15), (5, 20))


def spread(block):
    wide = block.astype(jnp.float32)
    columns = wide.shape[1]
    lane = lax.broadcasted_iota(jnp.int32, wide.shape, 1)
    right = jnp.where(lane == 0, 0.0, pltpu.roll(wide, 1, 1))
    left = jnp.where(lane == columns - 1, 0.0, pltpu.roll(wide, columns - 1, 1))
    return right.astype(block.dtype), block, left.astype(block.dtype)


def fill(taps, plane, row, block):
    channels = block.shape[0]
    for k, part in enumerate(spread(block)):
        taps[plane, row + 1, k * channels : (k + 1) * channels, :] = part


def clear_rim(taps):
    planes, rows, depth, columns = taps.shape
    for plane in range(planes):
        for row in (0, rows - 1):
            taps[plane, row] = jnp.zeros((depth, columns), taps.dtype)


def patch(taps, row):
    planes, _, depth, columns = taps.shape
    tall = []
    for plane in range(planes):
        tall.append(
            jnp.concatenate(
                [
                    taps[plane, pl.ds(row + r, 3)].reshape(3 * depth, columns)
                    for r in range(STEP)
                ],
                axis=1,
            )
        )
    return jnp.concatenate(tall, axis=0)


def ring_sizes():
    return 2, lax.axis_size("dp"), lax.axis_size("space") // 2


def copies_per_sum():
    pair, line, deep = ring_sizes()
    return 2 * (pair - 1 + line - 1 + deep - 1)


def sum_scratch(rows, columns):
    pair, line, deep = ring_sizes()
    return [
        pltpu.VMEM((line, deep, rows, columns), jnp.float32),
        pltpu.VMEM((line - 1, deep, rows, columns), jnp.float32),
        pltpu.VMEM((deep, rows, columns), jnp.float32),
        pltpu.VMEM((deep - 1, rows, columns), jnp.float32),
        pltpu.VMEM((pair, line, deep, rows, columns), jnp.float32),
        pltpu.SemaphoreType.DMA((copies_per_sum(),)),
        pltpu.SemaphoreType.DMA((copies_per_sum(),)),
    ]


class SumStages:
    def __init__(self, x, total, half, from_line, quarter, from_deep, full, sends, recvs):
        self.x, self.total, self.half, self.from_line = x, total, half, from_line
        self.quarter, self.from_deep, self.full = quarter, from_deep, full
        self.sends, self.recvs = sends, recvs
        self.pair, self.line, self.deep = ring_sizes()
        self.dp = lax.axis_index("dp")
        space = lax.axis_index("space")
        self.core, self.z = lax.rem(space, 2), space // 2
        self.partners = [(self.dp, self.z * 2 + 1 - self.core)]
        self.lines = [lax.rem(self.dp + t, self.line) for t in range(1, self.line)]
        self.deeps = [lax.rem(self.z + t, self.deep) for t in range(1, self.deep)]
        self.partners += [(p, space) for p in self.lines]
        self.partners += [(self.dp, p * 2 + self.core) for p in self.deeps]

    def greet(self, *more):
        barrier = pltpu.get_barrier_semaphore()
        others = [*self.partners, *more]
        for other in others:
            pl.semaphore_signal(
                barrier, inc=1, device_id=other, device_id_type=pl.DeviceIdType.MESH
            )
        pl.semaphore_wait(barrier, len(others))

    def copy(self, source, target, slot, other):
        return pltpu.make_async_remote_copy(
            src_ref=source,
            dst_ref=target,
            send_sem=self.sends.at[slot],
            recv_sem=self.recvs.at[slot],
            device_id=self.partners[other],
            device_id_type=pl.DeviceIdType.MESH,
        )

    def moves(self, stage):
        first_line, first_deep, second = 1, self.line, self.line + self.deep - 1
        mine = self.full.at[self.core]
        if stage == 0:
            return [self.copy(self.x.at[1 - self.core], self.half, 0, 0)]
        if stage == 1:
            return [
                self.copy(self.half.at[p], self.from_line.at[t], first_line + t, first_line + t)
                for t, p in enumerate(self.lines)
            ]
        if stage == 2:
            return [
                self.copy(self.quarter.at[p], self.from_deep.at[t], first_deep + t, first_deep + t)
                for t, p in enumerate(self.deeps)
            ]
        if stage == 3:
            own = mine.at[self.dp, self.z]
            return [
                self.copy(own, own, second + first_deep + t, first_deep + t)
                for t in range(len(self.deeps))
            ]
        if stage == 4:
            own = mine.at[self.dp]
            return [
                self.copy(own, own, second + first_line + t, first_line + t)
                for t in range(len(self.lines))
            ]
        return [self.copy(mine, mine, second, 0)]

    def run(self, stage):
        if stage > 0:
            for move in self.moves(stage - 1):
                move.wait()
        if stage == 1:
            self.half[...] += self.x[self.core]
        if stage == 2:
            value = self.half[self.dp]
            for t in range(len(self.lines)):
                value += self.from_line[t]
            self.quarter[...] = value
        if stage == 3:
            value = self.quarter[self.z]
            for t in range(len(self.deeps)):
                value += self.from_deep[t]
            self.full[self.core, self.dp, self.z] = value
        if stage < 6:
            for move in self.moves(stage):
                move.start()
        else:
            self.total[...] = self.full[...]


def fused_kernel(
    mid, w, back_w, bias, cot, x, act, out, small_total, total,
    taps, back_taps, gk, gp, lo, hi, glo, ghi, small,
    halo_sends, halo_recvs, grad_sends, grad_recvs, *scratch
):
    depth, rows, channels, columns = mid.shape
    outs = cot.shape[2]
    plane = 9 * channels
    steps = rows // STEP
    part = rows // PARTS
    space = lax.axis_index("space")
    dp = lax.axis_index("dp")
    last = lax.axis_size("space") - 1
    half = len(scratch) // 2
    wide = SumStages(x, total, *scratch[:half])
    late = SumStages(small, small_total, *scratch[half:])
    other = lax.rem(space + 2 * lax.rem(space, 2) + last, last + 1)
    wide.greet((dp, other))

    def push(source, target, send, recv, to):
        return pltpu.make_async_remote_copy(
            src_ref=source,
            dst_ref=target,
            send_sem=send,
            recv_sem=recv,
            device_id=(dp, to),
            device_id_type=pl.DeviceIdType.MESH,
        )

    def volume_down():
        return push(mid.at[0], hi, halo_sends.at[0], halo_recvs.at[0], space - 1)

    def volume_up():
        return push(mid.at[depth - 1], lo, halo_sends.at[1], halo_recvs.at[1], space + 1)

    def grad_down(n):
        at = pl.ds(n * part, part)
        return push(gp.at[0, at], ghi.at[at], grad_sends.at[0, n], grad_recvs.at[0, n], space - 1)

    def grad_up(n):
        at = pl.ds(n * part, part)
        return push(
            gp.at[depth - 1, at], glo.at[at], grad_sends.at[1, n], grad_recvs.at[1, n], space + 1
        )

    @pl.when(space > 0)
    def _():
        volume_down().start()

    @pl.when(space < last)
    def _():
        volume_up().start()

    wide.run(0)
    clear_rim(taps)
    clear_rim(back_taps)

    @pl.loop(0, rows, unroll=8)
    def _(row):
        for z in range(depth):
            fill(taps, z + 1, row, mid[z, row])

    def rim(target, plane_in, edge):
        @pl.when(space == (last if edge else 0))
        def _():
            plane_in[...] = jnp.zeros_like(plane_in)

        @pl.loop(0, rows, unroll=8)
        def _(row):
            fill(target, depth + 1 if edge else 0, row, plane_in[row])

    @pl.when(space > 0)
    def _():
        volume_down().wait_send()
        volume_up().wait_recv()

    @pl.when(space < last)
    def _():
        volume_up().wait_send()
        volume_down().wait_recv()

    rim(taps, lo, 0)
    rim(taps, hi, 1)
    gk[...] = jnp.zeros_like(gk)

    @pl.loop(0, steps)
    def _(step):
        for stage, at in FORWARD_AT:

            @pl.when(step == steps * at // 24)
            def _():
                wide.run(stage)

        row = step * STEP
        cells = patch(taps, row)
        pre = jnp.dot(w[...], cells, preferred_element_type=jnp.float32) + bias[...]
        grads = []
        for z in range(depth):
            line = []
            for r in range(STEP):
                v = pre[z * outs : (z + 1) * outs, r * columns : (r + 1) * columns]
                e = jnp.exp(-jnp.abs(v))
                soft = jnp.maximum(v, 0.0) + jnp.log(1.0 + e)
                sig = jnp.where(v >= 0.0, 1.0, e) / (1.0 + e)
                act[z, row + r] = (0.3 * v + 0.7 * soft).astype(act.dtype)
                g = (cot[z, row + r].astype(jnp.float32) * (0.3 + 0.7 * sig)).astype(gp.dtype)
                gp[z, row + r] = g
                fill(back_taps, z + 1, row + r, g)
                line.append(g)
            grads.append(jnp.concatenate(line, axis=1))
        grad = jnp.concatenate(grads, axis=0)
        ones = jnp.ones((16, STEP * columns), cells.dtype)
        gk[...] += lax.dot_general(
            jnp.concatenate([cells, ones], axis=0),
            grad,
            (((1,), (1,)), ((), ())),
            preferred_element_type=jnp.float32,
        )
        for n in range(PARTS):

            @pl.when(step == (n + 1) * steps // PARTS - 1)
            def _():
                @pl.when(space > 0)
                def _():
                    grad_down(n).start()

                @pl.when(space < last)
                def _():
                    grad_up(n).start()

    tall = 3 * plane
    ends = (depth + 2) * plane
    value = gk[0:tall, 0:outs]
    extra = gk[ends : ends + 8, 0:outs]
    for z in range(1, depth):
        value += gk[z * plane : z * plane + tall, z * outs : (z + 1) * outs]
        extra += gk[ends : ends + 8, z * outs : (z + 1) * outs]
    lines = small.size // columns
    small[...] = jnp.concatenate(
        [
            jnp.concatenate([value[: tall // 2], value[tall // 2 :]], axis=1),
            jnp.concatenate([extra, extra], axis=1),
            jnp.zeros((lines - tall // 2 - 8, columns), jnp.float32),
        ],
        axis=0,
    ).reshape(small.shape)
    late.run(0)

    @pl.when(space > 0)
    def _():
        for n in range(PARTS):
            grad_down(n).wait_send()
            grad_up(n).wait_recv()

    @pl.when(space < last)
    def _():
        for n in range(PARTS):
            grad_up(n).wait_send()
            grad_down(n).wait_recv()

    rim(back_taps, glo, 0)
    rim(back_taps, ghi, 1)

    @pl.loop(0, steps)
    def _(step):
        for stage, at in WIDE_AT:

            @pl.when(step == steps * at // 24)
            def _():
                wide.run(stage)

        for stage, at in BACKWARD_AT:

            @pl.when(step == steps * at // 24)
            def _():
                late.run(stage)

        row = step * STEP
        res = jnp.dot(back_w[...], patch(back_taps, row), preferred_element_type=jnp.float32)
        for z in range(depth):
            for r in range(STEP):
                out[z, row + r] = res[
                    z * channels : (z + 1) * channels, r * columns : (r + 1) * columns
                ].astype(out.dtype)

    wide.run(6)
    late.run(6)


def banded(w, depth):
    outs, width = w.shape[1:]
    flat = w.transpose(1, 0, 2).reshape(outs, 3 * width)
    lines = [
        jnp.pad(flat, ((0, 0), (z * width, (depth - 1 - z) * width))) for z in range(depth)
    ]
    return jnp.concatenate(lines, axis=0)


def local(volumes, kernel, bias, cotangent, finished_grads):
    volume = volumes[0].transpose(1, 2, 0, 3)
    cot = cotangent[0].transpose(1, 2, 0, 3)
    depth, rows, ins, columns = volume.shape
    outs = cot.shape[2]
    planes = depth + 2
    forward_w = banded(kernel.transpose(0, 3, 1, 2, 4).reshape(3, outs, 9 * ins), depth)
    backward_w = banded(
        kernel[::-1, ::-1, ::-1].transpose(0, 4, 1, 2, 3).reshape(3, ins, 9 * outs), depth
    )
    tall_bias = jnp.tile(bias, depth)[:, None]
    sizes = ring_sizes()
    devices = math.prod(sizes)

    def share(count):
        return 8 * math.ceil(count / (columns * devices * 8))

    entries = finished_grads.size
    parts = share(entries)
    flat = jnp.pad(finished_grads.reshape(-1), (0, parts * columns * devices - entries))
    tall = 27 * ins // 2
    small_parts = share((tall + 8) * columns)
    narrow = jnp.bfloat16
    act, gvol, small_sum, summed = pl.pallas_call(
        fused_kernel,
        out_shape=(
            jax.ShapeDtypeStruct(cot.shape, narrow),
            jax.ShapeDtypeStruct(volume.shape, narrow),
            jax.ShapeDtypeStruct((*sizes, small_parts, columns), jnp.float32),
            jax.ShapeDtypeStruct((*sizes, parts, columns), jnp.float32),
        ),
        in_specs=[VMEM] * 6,
        out_specs=(VMEM,) * 4,
        scratch_shapes=[
            pltpu.VMEM((planes, rows + 2, 3 * ins, columns), narrow),
            pltpu.VMEM((planes, rows + 2, 3 * outs, columns), narrow),
            pltpu.VMEM((planes * 9 * ins + 16, depth * outs), jnp.float32),
            pltpu.VMEM(cot.shape, narrow),
            pltpu.VMEM(volume.shape[1:], narrow),
            pltpu.VMEM(volume.shape[1:], narrow),
            pltpu.VMEM(cot.shape[1:], narrow),
            pltpu.VMEM(cot.shape[1:], narrow),
            pltpu.VMEM((*sizes, small_parts, columns), jnp.float32),
            pltpu.SemaphoreType.DMA((2,)),
            pltpu.SemaphoreType.DMA((2,)),
            pltpu.SemaphoreType.DMA((2, PARTS)),
            pltpu.SemaphoreType.DMA((2, PARTS)),
            *sum_scratch(parts, columns),
            *sum_scratch(small_parts, columns),
        ],
        compiler_params=pltpu.CompilerParams(
            vmem_limit_bytes=52 * 2**20, collective_id=0, has_side_effects=True
        ),
        name="fused",
    )(
        volume,
        forward_w,
        backward_w,
        tall_bias,
        cot,
        flat.reshape(*sizes, parts, columns),
    )
    count = lax.axis_size("dp") * lax.axis_size("space") * depth * rows * columns
    scale = 1.0 / math.sqrt(count)
    lines = small_sum.reshape(-1, columns)
    halves = [lines[:tall, h * outs : (h + 1) * outs] for h in range(2)]
    taps = jnp.concatenate(halves, axis=0).reshape(3, 3, 3, ins, outs)
    activations = act.transpose(2, 0, 1, 3)[None]
    grad_volumes = gvol.transpose(2, 0, 1, 3)[None]
    return (
        activations,
        grad_volumes,
        taps.transpose(0, 1, 2, 4, 3) * scale,
        lines[tall, :outs] * scale,
        summed.reshape(-1)[:entries],
    )


def solution(mesh):
    slab = P("dp", None, "space", None, None)
    return jax.shard_map(
        local,
        mesh=mesh,
        in_specs=(slab, P(), P(), slab, P("dp", "space", None)),
        out_specs=(slab, slab, P(), P(), P()),
        check_vma=False,
    )
```
